256 devices in a mesh: dp: 2 (over y_lo), ctx: 16 (over x, y_hi, core), tp: 8 (over z).
Axes of the slice: x: 4, y: 4 (y_hi: 2, y_lo: 2; y = y_hi * 2 + y_lo), z: 8, core: 2. Of those that a mesh axis runs over, the one named last changes fastest.
Arguments:
- q_prompt: bfloat16 [4, 3072, 16384], P('dp', 'ctx', 'tp'), parts along dimension 0, may hold values from -8 to 8
- k_prompt: bfloat16 [4, 3072, 1024], P('dp', 'ctx', 'tp'), parts along dimension 0, may hold values from -8 to 8
- v_prompt: bfloat16 [4, 3072, 1024], P('dp', 'ctx', 'tp'), parts along dimension 0, may hold values from -6 to 6
- q_follow: bfloat16 [4, 512, 16384], P('dp', 'ctx', 'tp'), parts along dimension 0, may hold values from -8 to 8
- k_follow: bfloat16 [4, 512, 1024], P('dp', 'ctx', 'tp'), parts along dimension 0, may hold values from -8 to 8
- v_follow: bfloat16 [4, 512, 1024], P('dp', 'ctx', 'tp'), parts along dimension 0, may hold values from -6 to 6
- lengths: int32 [4, 2], P('dp'), parts along dimension 0, may hold values from 256 to 3072, as said below
- block_order: int32 [4, 32], P('dp'), parts along dimension 0, may hold values from 0 to 31, as said below
Outputs:
- attn_prompt: bfloat16 [4, 3072, 16384], P('dp', 'ctx', 'tp'), parts along dimension 0
- attn_follow: bfloat16 [4, 512, 16384], P('dp', 'ctx', 'tp'), parts along dimension 0
The draws below stay inside these ranges and needn't reach their ends.
There are 2 independent parts, one for each index of `dp`. The reference program is written for one: setup_inputs(seed, part) draws one part's arguments, and reference() takes and returns one part's arrays. A program takes and returns all parts, laid end to end along the dimension named above; each array names one. Nothing has to cross between parts.
Inputs may be any that keep to these rules, and one draw needn't show every extreme that they name: In each part, one conversation drawn from the seed has lengths exactly 3072 and 512; every prompt length lies in 1536 to 3072, every follow-up length in 256 to 512. `block_order`: for each conversation, block slots 2 d and 2 d + 1 hold blocks b and 31 - b; every block appears once.
All inputs are finite; a program needn't handle non-finite values.
Results may differ from the reference program's by a relative error of at most 0.033.
Values may be sent and summed in bfloat16 or wider, within the bound.
A program may use at most 64 MiB of HBM per device.

```python
import math
import jax
import jax.numpy as jnp
from jax import lax

HEADS = 128
KV_HEADS = 8
HEAD_DIM = 128
CONV = 2
PROMPT = 3072
FOLLOW = 512
NBLK = 32
BLOCK = 96


def draw_q_prompt(key, part):
    key = jax.random.fold_in(key, 21)
    return jnp.clip(jax.random.normal(key, (CONV, PROMPT, HEADS * HEAD_DIM), jnp.float32), -6.0, 6.0).astype(jnp.bfloat16)


def draw_k_prompt(key, part):
    key = jax.random.fold_in(key, 22)
    return jnp.clip(jax.random.normal(key, (CONV, PROMPT, KV_HEADS * HEAD_DIM), jnp.float32), -6.0, 6.0).astype(jnp.bfloat16)


def draw_q_follow(key, part):
    key = jax.random.fold_in(key, 23)
    return jnp.clip(jax.random.normal(key, (CONV, FOLLOW, HEADS * HEAD_DIM), jnp.float32), -6.0, 6.0).astype(jnp.bfloat16)


def draw_k_follow(key, part):
    key = jax.random.fold_in(key, 24)
    return jnp.clip(jax.random.normal(key, (CONV, FOLLOW, KV_HEADS * HEAD_DIM), jnp.float32), -6.0, 6.0).astype(jnp.bfloat16)


def draw_lengths(key, part):
    key = jax.random.fold_in(key, 31)
    first_key, second_key, third_key = jax.random.split(key, 3)
    longest = jax.random.randint(first_key, (), 0, CONV)
    prompt_len = jax.random.randint(second_key, (CONV,), PROMPT // 2, PROMPT + 1)
    follow_len = jax.random.randint(third_key, (CONV,), FOLLOW // 2, FOLLOW + 1)
    chosen = jnp.arange(CONV) == longest
    return jnp.stack([jnp.where(chosen, PROMPT, prompt_len), jnp.where(chosen, FOLLOW, follow_len)], axis=1).astype(jnp.int32)


def pick_order(one_key):
    return jax.random.permutation(one_key, NBLK // 2)


def draw_block_order(key, part):
    key = jax.random.fold_in(key, 41)
    conv_keys = jax.random.split(key, CONV)
    orders = jax.vmap(pick_order)(conv_keys).astype(jnp.int32)
    return jnp.stack([orders, NBLK - 1 - orders], axis=2).reshape(CONV, NBLK).astype(jnp.int32)


def level_of(key, dims, cuts, least, top_value):
    def one(axis_at, parts):
        steps = jax.random.uniform(jax.random.fold_in(jax.random.fold_in(key, 6), axis_at), (parts,), jnp.float32, least / len(cuts), top_value / len(cuts))
        return jnp.repeat(jnp.exp(steps), dims[axis_at] // parts).reshape((-1,) + (1,) * (len(dims) - axis_at - 1))

    loudness = one(*cuts[0])
    for cut in cuts[1:]:
        loudness = loudness * one(*cut)
    return loudness


def noise(key, shape, deviation, most, pieces=(), held_as=jnp.bfloat16):
    values = deviation * jax.random.normal(key, shape, jnp.float32)
    if pieces:
        values = values * level_of(key, shape, pieces, -0.22, 0.18)
    return jnp.clip(values, -most, most).astype(held_as)


def setup_inputs(seed: int = 0, part: int = 0) -> dict:
    seeds = jax.random.split(jax.random.key(seed), 9)
    part_keys = jax.random.split(jax.random.fold_in(seeds[8], part), 9)
    return {
        "q_prompt": draw_q_prompt(jax.random.fold_in(jax.random.fold_in(seeds[8], part), 71), part),
        "k_prompt": draw_k_prompt(jax.random.fold_in(jax.random.fold_in(seeds[8], part), 71), part),
        "v_prompt": noise(part_keys[2], (CONV, PROMPT, KV_HEADS * HEAD_DIM), 1.0, 6.0, ((1, 16), (2, 8))),
        "q_follow": draw_q_follow(jax.random.fold_in(jax.random.fold_in(seeds[8], part), 71), part),
        "k_follow": draw_k_follow(jax.random.fold_in(jax.random.fold_in(seeds[8], part), 71), part),
        "v_follow": noise(part_keys[5], (CONV, FOLLOW, KV_HEADS * HEAD_DIM), 1.0, 6.0, ((1, 16), (2, 8))),
        "lengths": draw_lengths(jax.random.fold_in(jax.random.fold_in(seeds[8], part), 71), part),
        "block_order": draw_block_order(jax.random.fold_in(jax.random.fold_in(seeds[8], part), 71), part),
    }


def slot_positions(order_row):
    slot_ids = jnp.arange(PROMPT, dtype=jnp.int32)
    return order_row[slot_ids // BLOCK].astype(jnp.int32) * BLOCK + slot_ids % BLOCK

def attend(query, key_rows, value_rows, visible, query_live):
    row_count = query.shape[0]
    group_size = HEADS // KV_HEADS
    query4 = query.reshape(row_count, KV_HEADS, group_size, HEAD_DIM).transpose(1, 0, 2, 3)
    keys3 = key_rows.reshape(key_rows.shape[0], KV_HEADS, HEAD_DIM).transpose(1, 0, 2)
    values3 = value_rows.reshape(value_rows.shape[0], KV_HEADS, HEAD_DIM).transpose(1, 0, 2)

    def one_head(operands):
        query_head, key_head, value_head = operands
        scores = jnp.einsum('rgd,kd->grk', query_head.astype(jnp.float32), key_head.astype(jnp.float32)) * (1.0 / math.sqrt(HEAD_DIM))
        scores = jnp.where(visible[None], scores, jnp.float32(-1e+30))
        highest = lax.optimization_barrier(jnp.max(scores, axis=-1))
        weights = jnp.where(visible[None], jnp.exp(scores - highest[..., None]), jnp.float32(0.0))
        denominator = lax.optimization_barrier(jnp.sum(weights, axis=-1))
        rounded = lax.optimization_barrier(weights.astype(jnp.bfloat16)).astype(jnp.float32)
        summed = jnp.einsum('grk,kd->grd', rounded, value_head.astype(jnp.float32))
        return summed / denominator[..., None]
    heads_out = lax.map(one_head, (query4, keys3, values3))
    result = heads_out.transpose(2, 0, 1, 3).reshape(row_count, HEADS * HEAD_DIM)
    return jnp.where(query_live[:, None], result, jnp.float32(0.0)).astype(jnp.bfloat16)

def reference(q_prompt, k_prompt, v_prompt, q_follow, k_follow, v_follow, lengths, block_order):
    prompt_outs = []
    follow_outs = []
    for c in range(CONV):
        position = slot_positions(block_order[c])
        prompt_live = position < lengths[c, 0]
        visible = (position[None, :] <= position[:, None]) & prompt_live[None, :]
        prompt_outs.append(attend(q_prompt[c], k_prompt[c], v_prompt[c], visible, prompt_live))
        follow_ids = jnp.arange(FOLLOW, dtype=jnp.int32)
        follow_live = follow_ids < lengths[c, 1]
        cached = jnp.broadcast_to(prompt_live[None, :], (FOLLOW, PROMPT))
        causal = (follow_ids[None, :] <= follow_ids[:, None]) & follow_live[None, :]
        follow_visible = jnp.concatenate([cached, causal], axis=1)
        all_keys = jnp.concatenate([k_prompt[c], k_follow[c]], axis=0)
        all_values = jnp.concatenate([v_prompt[c], v_follow[c]], axis=0)
        follow_outs.append(attend(q_follow[c], all_keys, all_values, follow_visible, follow_live))
    return (jnp.stack(prompt_outs), jnp.stack(follow_outs))
```

```python
import functools
import math

import jax
import jax.numpy as jnp
from jax import lax
from jax.experimental import pallas as pl
from jax.experimental.pallas import tpu as pltpu
from jax.sharding import PartitionSpec as P

HEAD_DIM = 128
CONV = 2
HALF = 96
FOLLOW = 32
CHUNK = 2 * HALF + FOLLOW
GROUP = 16
CTX = 16
PROMPT_TILE = 384
PROMPT_HEADS = PROMPT_TILE // HALF
FOLLOW_TILE = 256
FOLLOW_HEADS = FOLLOW_TILE // FOLLOW
TILE_UNITS = 4
TILES = 5
HIDE = -1e30
FLOOR = -1e20
SCALE = math.log2(math.e) / math.sqrt(HEAD_DIM)
MESH = pl.DeviceIdType.MESH

SLOTS = (
    (0, 0, 0), (0, 0, 1), (3, 0, 0), (3, 0, 1), (1, 0, 0), (1, 0, 1), (0, 1, 0), (0, 1, 1),
    (3, 1, 0), (3, 1, 1), (1, 1, 0), (1, 1, 1), (2, 0, 0), (2, 0, 1), (2, 1, 0), (2, 1, 1),
)
SLOT_OF = {place: s for s, place in enumerate(SLOTS)}

OWN_SENDS = (
    ((0, 0, 0), 0, 2, (0, 1, 0), (0, 1, 0)),
    ((0, 0, 0), 0, 2, (1, 0, 0), (3, 0, 0)),
    ((0, 0, 0), 0, 2, (3, 0, 0), (1, 0, 0)),
    ((0, 0, 0), 0, 2, (0, 0, 1), (0, 0, 1)),
)
FORWARDS = {
    (0, 1, 0): (
        ((0, 1, 0), 0, 2, (1, 0, 0), (3, 1, 0)),
        ((0, 1, 0), 0, 2, (3, 0, 0), (1, 1, 0)),
        ((0, 1, 0), 0, 2, (0, 0, 1), (0, 1, 1)),
    ),
    (3, 0, 0): (
        ((3, 0, 0), 0, 1, (1, 0, 0), (2, 0, 0)),
        ((3, 0, 0), 0, 2, (0, 0, 1), (3, 0, 1)),
    ),
    (1, 0, 0): (
        ((1, 0, 0), 1, 1, (3, 0, 0), (2, 0, 0)),
        ((1, 0, 0), 0, 2, (0, 0, 1), (1, 0, 1)),
    ),
    (3, 1, 0): (
        ((3, 1, 0), 0, 1, (1, 0, 0), (2, 1, 0)),
        ((3, 1, 0), 0, 2, (0, 0, 1), (3, 1, 1)),
    ),
    (1, 1, 0): (
        ((1, 1, 0), 1, 1, (3, 0, 0), (2, 1, 0)),
        ((1, 1, 0), 0, 2, (0, 0, 1), (1, 1, 1)),
    ),
    (2, 0, 0): (((2, 0, 0), 0, 2, (0, 0, 1), (2, 0, 1)),),
    (2, 1, 0): (((2, 1, 0), 0, 2, (0, 0, 1), (2, 1, 1)),),
}
ALL_SENDS = OWN_SENDS + tuple(send for sends in FORWARDS.values() for send in sends)
SEND_INDEX = {send: n for n, send in enumerate(ALL_SENDS)}


def scores_of(query, keys):
    return lax.dot_general(
        query, keys, (((1,), (1,)), ((), ())), preferred_element_type=jnp.float32
    )


def absorb(query, keys, values, highest, total):
    scores = scores_of(query, keys)
    width = scores.shape[1]
    top = jnp.maximum(jnp.max(scores, axis=1, keepdims=True), FLOOR)
    if highest is None:
        top = jnp.broadcast_to(top, (scores.shape[0], 128))
    else:
        top = jnp.maximum(highest, top)
    weights = jnp.exp2((scores - jnp.tile(top, (1, width // 128))) * SCALE).astype(jnp.bfloat16)
    beside = jnp.concatenate([values, jnp.ones_like(values)], axis=1)
    added = jnp.dot(weights, beside, preferred_element_type=jnp.float32)
    if highest is not None:
        factor = jnp.exp2((highest - top) * SCALE)
        added = added + total * jnp.tile(factor, (1, 2))
    return top, added


def kernel(
    lengths, order, q_hbm, k_hbm, v_hbm, qf_hbm, kf_hbm, vf_hbm,
    out_hbm, outf_hbm,
    q_ref, k_ref, v_ref, qf_ref, kf_ref, vf_ref, out_ref, outf_ref,
    held0, held1, f_mask, unit_mask, p_query_mask, f_query_mask,
    high_top, high_total, step_top, step_total, f_top, f_total,
    in_sem, out_sem, send_sem, recv_sem,
):
    held = (held0, held1)
    me = lax.axis_index("ctx")
    my_x, my_y, my_k = me // 4, (me // 2) % 2, me % 2

    def device_at(offset):
        dx, dy, dk = offset
        return (((my_x + dx) % 4) * 2 + (my_y + dy) % 2) * 2 + (my_k + dk) % 2

    loads = []
    for c in range(CONV):
        for n, (src, dst) in enumerate(
            ((k_hbm, k_ref), (v_hbm, v_ref), (kf_hbm, kf_ref), (vf_hbm, vf_ref))
        ):
            loads.append(pltpu.make_async_copy(src.at[c], dst.at[c], in_sem.at[4 * c + n]))
    load_q = [
        pltpu.make_async_copy(q_hbm.at[c], q_ref.at[c], in_sem.at[8 + c]) for c in range(CONV)
    ]
    load_qf = pltpu.make_async_copy(qf_hbm, qf_ref, in_sem.at[10])
    for load in loads:
        load.start()
    load_qf.start()
    for load in load_q:
        load.start()

    barrier = pltpu.get_barrier_semaphore()
    for send in OWN_SENDS:
        pl.semaphore_signal(barrier, inc=1, device_id={"ctx": device_at(send[3])}, device_id_type=MESH)
    pl.semaphore_wait(barrier, len(OWN_SENDS))

    def copy_of(c, send):
        source, part, parts, target, landing = send
        where = pl.ds(part, parts)
        return pltpu.make_async_remote_copy(
            src_ref=held[c].at[SLOT_OF[source], where],
            dst_ref=held[c].at[SLOT_OF[landing], where],
            send_sem=send_sem.at[c, SEND_INDEX[send]],
            recv_sem=recv_sem.at[c, SEND_INDEX[send]],
            device_id={"ctx": device_at(target)},
            device_id_type=MESH,
        )

    block = [[order[c, 2 * me + half] for half in range(2)] for c in range(CONV)]
    low_half = [jnp.where(block[c][0] < block[c][1], 0, 1) for c in range(CONV)]
    low_block = [jnp.minimum(block[c][0], block[c][1]) for c in range(CONV)]
    for c in range(CONV):
        for load in loads[4 * c : 4 * c + 4]:
            load.wait()
        for part, (rows, later) in enumerate(((k_ref, kf_ref), (v_ref, vf_ref))):
            first, second = rows[c, 0], rows[c, 1]
            held[c][0, part, 0:HALF, :] = jnp.where(low_half[c] == 0, first, second)
            held[c][0, part, HALF : 2 * HALF, :] = jnp.where(low_half[c] == 0, second, first)
            held[c][0, part, 2 * HALF : CHUNK, :] = later[c]
        for send in OWN_SENDS:
            copy_of(c, send).start()

    def arrive(c, slot):
        for send in ALL_SENDS:
            if send[4] == slot:
                copy_of(c, send).wait_recv()
        for send in FORWARDS.get(slot, ()):
            copy_of(c, send).start()

    def iotas(rows):
        return (
            lax.broadcasted_iota(jnp.int32, (rows, 128), 0),
            lax.broadcasted_iota(jnp.int32, (rows, 128), 1),
        )

    row, lane = iotas(HALF)
    unit_mask[0] = jnp.zeros((HALF, 128), jnp.bfloat16)
    unit_mask[1] = jnp.where(lane == row, 1.0, 0.0).astype(jnp.bfloat16)
    unit_mask[2] = jnp.where(lane == HALF, 1.0, 0.0).astype(jnp.bfloat16)
    hidden = jnp.where(((lane > row) & (lane < HALF)) | (lane == HALF), HIDE, 0.0).astype(jnp.bfloat16)
    for h in range(PROMPT_HEADS):
        p_query_mask[h * HALF : (h + 1) * HALF, :] = hidden
    row, lane = iotas(FOLLOW)
    hidden = jnp.where(((lane > row) & (lane < FOLLOW)) | (lane == FOLLOW), HIDE, 0.0).astype(jnp.bfloat16)
    for h in range(FOLLOW_HEADS):
        f_query_mask[h * FOLLOW : (h + 1) * FOLLOW, :] = hidden
    for c in range(CONV):
        for slot, offset in enumerate(SLOTS):
            owner = device_at(offset)
            lower = jnp.minimum(order[c, 2 * owner], order[c, 2 * owner + 1])
            row, lane = iotas(HALF)
            for half, number in enumerate((lower, 31 - lower)):
                dead = (row + number * HALF >= lengths[c, 0]) & (lane == FOLLOW)
                f_mask[c, slot, half * HALF : (half + 1) * HALF, :] = jnp.where(dead, 1.0, 0.0).astype(
                    jnp.bfloat16
                )
            row, lane = iotas(FOLLOW)
            position = row + owner * FOLLOW
            if slot == 0:
                seen = (lane == row) | ((position >= lengths[c, 1]) & (lane == FOLLOW))
            else:
                last = jnp.minimum(lengths[c, 1], me * FOLLOW)
                seen = (position >= last) & (lane == FOLLOW)
            f_mask[c, slot, 2 * HALF : CHUNK, :] = jnp.where(seen, 1.0, 0.0).astype(jnp.bfloat16)

    def place(c, number):
        found = jnp.int32(0)
        for slot, offset in enumerate(SLOTS):
            owner = device_at(offset)
            lower = jnp.minimum(order[c, 2 * owner], order[c, 2 * owner + 1])
            found = jnp.where(lower == number, slot, found)
        return found

    def prompt_query(c, half, tile):
        start = tile * (PROMPT_HEADS * HEAD_DIM)
        return jnp.concatenate(
            [
                q_ref[c, half, :, pl.ds(pl.multiple_of(start + h * HEAD_DIM, HEAD_DIM), HEAD_DIM)]
                for h in range(PROMPT_HEADS)
            ],
            axis=0,
        )

    def high_on_low(c, slots, first):
        keys = [held[c][s, 0, 0:HALF, :] for s in slots]
        values = [held[c][s, 1, 0:HALF, :] for s in slots]

        def step(tile, carry):
            rows = pl.ds(pl.multiple_of(tile * PROMPT_TILE, PROMPT_TILE), PROMPT_TILE)
            query = prompt_query(c, 1 - low_half[c], tile)
            top, total = absorb(
                query,
                jnp.concatenate([held[c][s, 0, 0:HALF, :] for s in slots], axis=0),
                jnp.concatenate([held[c][s, 1, 0:HALF, :] for s in slots], axis=0),
                None if first else high_top[rows, :],
                None if first else high_total[rows, :],
            )
            high_top[rows, :] = top
            high_total[rows, :] = total
            return carry

        lax.fori_loop(0, GROUP // PROMPT_HEADS, step, 0)

    def follow(c, slots, first):
        def step(tile, carry):
            rows = pl.ds(pl.multiple_of(tile * FOLLOW_TILE, FOLLOW_TILE), FOLLOW_TILE)
            start = tile * (FOLLOW_HEADS * HEAD_DIM)
            query = jnp.concatenate(
                [
                    qf_ref[c, :, pl.ds(pl.multiple_of(start + h * HEAD_DIM, HEAD_DIM), HEAD_DIM)]
                    for h in range(FOLLOW_HEADS)
                ],
                axis=0,
            )
            query = jnp.concatenate([query, f_query_mask[...]], axis=1)
            keys = jnp.concatenate(
                [jnp.concatenate([held[c][s, 0], f_mask[c, s]], axis=1) for s in slots], axis=0
            )
            top, total = absorb(
                query,
                keys,
                jnp.concatenate([held[c][s, 1] for s in slots], axis=0),
                None if first else f_top[rows, :],
                None if first else f_total[rows, :],
            )
            f_top[rows, :] = top
            f_total[rows, :] = total
            return carry

        lax.fori_loop(0, GROUP // FOLLOW_HEADS, step, 0)

    def finish_follow(c):
        live = lax.broadcasted_iota(jnp.int32, (FOLLOW, HEAD_DIM), 0) + me * FOLLOW < lengths[c, 1]
        for h in range(GROUP):
            rows = pl.ds(h * FOLLOW, FOLLOW)
            result = f_total[rows, 0:HEAD_DIM] / f_total[rows, HEAD_DIM:]
            outf_ref[c, :, h * HEAD_DIM : (h + 1) * HEAD_DIM] = jnp.where(live, result, 0.0).astype(
                jnp.bfloat16
            )

    def rest(c):
        mine = low_block[c]
        low_tiles = mine // TILE_UNITS + 1

        plan = []
        for t in range(TILES):
            is_high = jnp.where(low_tiles <= t, 1, 0)
            units = []
            for w in range(TILE_UNITS):
                ahead = jnp.where(
                    is_high == 1,
                    15 - (TILE_UNITS * (t - low_tiles) + w) - mine,
                    mine - (TILE_UNITS * t + w),
                )
                number = jnp.where(is_high == 1, mine + ahead, mine - ahead)
                number = jnp.minimum(jnp.maximum(number, 0), CTX - 1)
                kind = jnp.where(ahead > 0, 0, jnp.where(ahead == 0, 1, 2))
                units.append((place(c, number), kind))
            half = jnp.where(is_high == 1, 1 - low_half[c], low_half[c])
            before = 0 if t == 0 else jnp.where(low_tiles == t, 1, t + 1)
            plan.append((is_high, half, before, units))

        def step(tile, carry):
            rows = pl.ds(pl.multiple_of(tile * PROMPT_TILE, PROMPT_TILE), PROMPT_TILE)
            step_top[0] = jnp.full((PROMPT_TILE, 128), FLOOR, jnp.float32)
            step_total[0] = jnp.zeros((PROMPT_TILE, 2 * HEAD_DIM), jnp.float32)
            step_top[1] = high_top[rows, :]
            step_total[1] = high_total[rows, :]
            for t, (is_high, half, before, units) in enumerate(plan):
                keys, values = [], []
                for slot, kind in units:
                    rows_of = [
                        jnp.where(
                            is_high == 1,
                            held[c][slot, part, HALF : 2 * HALF, :],
                            held[c][slot, part, 0:HALF, :],
                        )
                        for part in range(2)
                    ]
                    keys.append(jnp.concatenate([rows_of[0], unit_mask[kind]], axis=1))
                    values.append(rows_of[1])
                query = jnp.concatenate([prompt_query(c, half, tile), p_query_mask[...]], axis=1)
                top, total = absorb(
                    query,
                    jnp.concatenate(keys, axis=0),
                    jnp.concatenate(values, axis=0),
                    step_top[before],
                    step_total[before],
                )
                step_top[t + 2] = top
                step_total[t + 2] = total
            for half in range(2):
                last = jnp.where(low_half[c] == half, low_tiles + 1, TILES + 1)
                position = (
                    lax.broadcasted_iota(jnp.int32, (HALF, HEAD_DIM), 0) + block[c][half] * HALF
                )
                live = position < lengths[c, 0]
                for h in range(PROMPT_HEADS):
                    some = pl.ds(h * HALF, HALF)
                    result = step_total[last, some, 0:HEAD_DIM] / step_total[last, some, HEAD_DIM:]
                    start = pl.multiple_of((tile * PROMPT_HEADS + h) * HEAD_DIM, HEAD_DIM)
                    out_ref[c, half, :, pl.ds(start, HEAD_DIM)] = jnp.where(
                        live, result, 0.0
                    ).astype(jnp.bfloat16)
            return carry

        lax.fori_loop(0, GROUP // PROMPT_HEADS, step, 0)

    stores = []

    def store(src, dst, n):
        copy = pltpu.make_async_copy(src, dst, out_sem.at[n])
        copy.start()
        stores.append(copy)

    schedule(arrive, high_on_low, follow, finish_follow, rest, store, load_q, load_qf,
             out_ref, out_hbm, outf_ref, outf_hbm)
    for c in range(CONV):
        for send in ALL_SENDS:
            copy_of(c, send).wait_send()
    for copy in stores:
        copy.wait()


def schedule(arrive, high_on_low, follow, finish_follow, rest, store, load_q, load_qf,
             out_ref, out_hbm, outf_ref, outf_hbm):
    load_qf.wait()
    for load in load_q:
        load.wait()
    for c in range(CONV):
        for slot in ((0, 0, 1), (3, 0, 0), (1, 0, 0), (0, 1, 0), (3, 0, 1), (1, 0, 1), (0, 1, 1)):
            arrive(c, slot)
        follow(c, (0, 1, 2, 3), True)
        follow(c, (4, 5, 6, 7), False)
        for slot in ((3, 1, 0), (1, 1, 0), (2, 0, 0)):
            arrive(c, slot)
        high_on_low(c, (0, 1, 2, 3, 4, 5, 6, 7), True)
        for slot in ((2, 1, 0), (3, 1, 1), (1, 1, 1), (2, 0, 1), (2, 1, 1)):
            arrive(c, slot)
        high_on_low(c, (8, 9, 10, 11, 12, 13, 14, 15), False)
        follow(c, (8, 9, 10, 11), False)
        follow(c, (12, 13, 14, 15), False)
        finish_follow(c)
        store(outf_ref.at[c], outf_hbm.at[c], 2 + c)
        rest(c)
        store(out_ref.at[c], out_hbm.at[c], c)


def on_device(q_prompt, k_prompt, v_prompt, q_follow, k_follow, v_follow, lengths, block_order):
    width = GROUP * HEAD_DIM
    any_space = pl.BlockSpec(memory_space=pl.ANY)
    smem = pl.BlockSpec(memory_space=pltpu.SMEM)
    bf16, f32 = jnp.bfloat16, jnp.float32
    halves = (CONV, 2, HALF)
    out, out_follow = pl.pallas_call(
        kernel,
        out_shape=(
            jax.ShapeDtypeStruct(halves + (width,), bf16),
            jax.ShapeDtypeStruct((CONV, FOLLOW, width), bf16),
        ),
        in_specs=[smem, smem] + [any_space] * 6,
        out_specs=(any_space, any_space),
        scratch_shapes=[
            pltpu.VMEM(halves + (width,), bf16),
            pltpu.VMEM(halves + (HEAD_DIM,), bf16),
            pltpu.VMEM(halves + (HEAD_DIM,), bf16),
            pltpu.VMEM((CONV, FOLLOW, width), bf16),
            pltpu.VMEM((CONV, FOLLOW, HEAD_DIM), bf16),
            pltpu.VMEM((CONV, FOLLOW, HEAD_DIM), bf16),
            pltpu.VMEM(halves + (width,), bf16),
            pltpu.VMEM((CONV, FOLLOW, width), bf16),
            pltpu.VMEM((CTX, 2, CHUNK, HEAD_DIM), bf16),
            pltpu.VMEM((CTX, 2, CHUNK, HEAD_DIM), bf16),
            pltpu.VMEM((CONV, CTX, CHUNK, HEAD_DIM), bf16),
            pltpu.VMEM((3, HALF, HEAD_DIM), bf16),
            pltpu.VMEM((PROMPT_TILE, HEAD_DIM), bf16),
            pltpu.VMEM((FOLLOW_TILE, HEAD_DIM), bf16),
            pltpu.VMEM((GROUP * HALF, HEAD_DIM), f32),
            pltpu.VMEM((GROUP * HALF, 2 * HEAD_DIM), f32),
            pltpu.VMEM((TILES + 2, PROMPT_TILE, HEAD_DIM), f32),
            pltpu.VMEM((TILES + 2, PROMPT_TILE, 2 * HEAD_DIM), f32),
            pltpu.VMEM((GROUP * FOLLOW, HEAD_DIM), f32),
            pltpu.VMEM((GROUP * FOLLOW, 2 * HEAD_DIM), f32),
            pltpu.SemaphoreType.DMA((11,)),
            pltpu.SemaphoreType.DMA((4,)),
            pltpu.SemaphoreType.DMA((CONV, len(ALL_SENDS))),
            pltpu.SemaphoreType.DMA((CONV, len(ALL_SENDS))),
        ],
        compiler_params=pltpu.CompilerParams(
            collective_id=0, has_side_effects=True, vmem_limit_bytes=48 << 20
        ),
        cost_estimate=pl.CostEstimate(
            flops=7_400_000_000, bytes_accessed=8_000_000, transcendentals=15_000_000
        ),
    )(
        lengths,
        block_order,
        q_prompt.reshape(halves + (width,)),
        k_prompt.reshape(halves + (HEAD_DIM,)),
        v_prompt.reshape(halves + (HEAD_DIM,)),
        q_follow,
        k_follow,
        v_follow,
    )
    return out.reshape(q_prompt.shape), out_follow


def solution(mesh):
    return jax.shard_map(
        on_device,
        mesh=mesh,
        in_specs=(P("dp", "ctx", "tp"),) * 6 + (P("dp", None), P("dp", None)),
        out_specs=(P("dp", "ctx", "tp"), P("dp", "ctx", "tp")),
        check_vma=False,
    )
```

```python
import functools
import math

import jax
import jax.numpy as jnp
from jax import lax
from jax.experimental import pallas as pl
from jax.experimental.pallas import tpu as pltpu
from jax.sharding import PartitionSpec as P

HEAD_DIM = 128
CONV = 2
HALF = 96
FOLLOW = 32
CHUNK = 2 * HALF + FOLLOW
GROUP = 16
CTX = 16
PROMPT_TILE = 384
PROMPT_HEADS = PROMPT_TILE // HALF
FOLLOW_TILE = 256
FOLLOW_HEADS = FOLLOW_TILE // FOLLOW
REST_TILES = (8, 8, 4)
HIDE = -1e30
FLOOR = -1e20
SCALE = math.log2(math.e) / math.sqrt(HEAD_DIM)
MESH = pl.DeviceIdType.MESH

SLOTS = (
    (0, 0, 0), (0, 0, 1), (3, 0, 0), (3, 0, 1), (1, 0, 0), (1, 0, 1), (0, 1, 0), (0, 1, 1),
    (3, 1, 0), (3, 1, 1), (1, 1, 0), (1, 1, 1), (2, 0, 0), (2, 0, 1), (2, 1, 0), (2, 1, 1),
)
SLOT_OF = {place: s for s, place in enumerate(SLOTS)}

OWN_SENDS = (
    ((0, 0, 0), 0, 2, (0, 1, 0), (0, 1, 0)),
    ((0, 0, 0), 0, 2, (1, 0, 0), (3, 0, 0)),
    ((0, 0, 0), 0, 2, (3, 0, 0), (1, 0, 0)),
    ((0, 0, 0), 0, 2, (0, 0, 1), (0, 0, 1)),
)
FORWARDS = {
    (0, 1, 0): (
        ((0, 1, 0), 0, 2, (1, 0, 0), (3, 1, 0)),
        ((0, 1, 0), 0, 2, (3, 0, 0), (1, 1, 0)),
        ((0, 1, 0), 0, 2, (0, 0, 1), (0, 1, 1)),
    ),
    (3, 0, 0): (
        ((3, 0, 0), 0, 1, (1, 0, 0), (2, 0, 0)),
        ((3, 0, 0), 0, 2, (0, 0, 1), (3, 0, 1)),
    ),
    (1, 0, 0): (
        ((1, 0, 0), 1, 1, (3, 0, 0), (2, 0, 0)),
        ((1, 0, 0), 0, 2, (0, 0, 1), (1, 0, 1)),
    ),
    (3, 1, 0): (
        ((3, 1, 0), 0, 1, (1, 0, 0), (2, 1, 0)),
        ((3, 1, 0), 0, 2, (0, 0, 1), (3, 1, 1)),
    ),
    (1, 1, 0): (
        ((1, 1, 0), 1, 1, (3, 0, 0), (2, 1, 0)),
        ((1, 1, 0), 0, 2, (0, 0, 1), (1, 1, 1)),
    ),
    (2, 0, 0): (((2, 0, 0), 0, 2, (0, 0, 1), (2, 0, 1)),),
    (2, 1, 0): (((2, 1, 0), 0, 2, (0, 0, 1), (2, 1, 1)),),
}
ALL_SENDS = OWN_SENDS + tuple(send for sends in FORWARDS.values() for send in sends)
SEND_INDEX = {send: n for n, send in enumerate(ALL_SENDS)}


def scores_of(query, keys):
    return lax.dot_general(
        query, keys, (((1,), (1,)), ((), ())), preferred_element_type=jnp.float32
    )


def weigh(scores, highest):
    top = jnp.maximum(jnp.max(scores, axis=1, keepdims=True), FLOOR)
    if highest is None:
        top = jnp.broadcast_to(top, (scores.shape[0], 128))
        factor = None
    else:
        top = jnp.maximum(highest, top)
        factor = jnp.exp2((highest - top) * SCALE)
    width = scores.shape[1]
    spread = jnp.tile(top, (1, -(-width // 128)))[:, :width]
    return top, jnp.exp2((scores - spread) * SCALE).astype(jnp.bfloat16), factor


def run(items):
    steps, calls = [], [[]]
    for item in items:
        if callable(item):
            calls[-1].append(item)
        else:
            steps.append(item)
            calls.append([])

    def begin(n):
        for call in calls[n]:
            call()
        return scores_of(steps[n][0](), steps[n][1]())

    ahead = begin(0)
    for n, (_, _, values, before, after) in enumerate(steps):
        scores = ahead
        if n + 1 < len(steps):
            ahead = begin(n + 1)
        highest, total = before()
        top, weights, factor = weigh(scores, highest)
        rows = values()
        added = jnp.dot(
            weights,
            jnp.concatenate([rows, jnp.ones_like(rows)], axis=1),
            preferred_element_type=jnp.float32,
        )
        if total is not None:
            added = added + total * jnp.tile(factor, (1, 2))
        after(top, added)
    for call in calls[-1]:
        call()


def kernel(
    lengths, order, q_hbm, k_hbm, v_hbm, qf_hbm, kf_hbm, vf_hbm,
    out_hbm, outf_hbm,
    q_ref, k_ref, v_ref, qf_ref, kf_ref, vf_ref, out_ref, outf_ref,
    held0, held1, f_mask, unit_mask, p_query_mask, f_query_mask,
    step_top, step_total, f_top, f_total,
    in_sem, out_sem, send_sem, recv_sem,
):
    held = (held0, held1)
    me = lax.axis_index("ctx")
    my_x, my_y, my_k = me // 4, lax.rem(me // 2, 2), lax.rem(me, 2)

    devices = {
        (dx, dy, dk): (lax.rem(my_x + dx, 4) * 2 + lax.rem(my_y + dy, 2)) * 2 + lax.rem(my_k + dk, 2)
        for dx, dy, dk in SLOTS
    }

    barrier = pltpu.get_barrier_semaphore()
    for send in OWN_SENDS:
        pl.semaphore_signal(barrier, inc=1, device_id={"ctx": devices[send[3]]}, device_id_type=MESH)

    loads = []
    for c in range(CONV):
        for n, (src, dst) in enumerate(
            ((k_hbm, k_ref), (v_hbm, v_ref), (kf_hbm, kf_ref), (vf_hbm, vf_ref))
        ):
            loads.append(pltpu.make_async_copy(src.at[c], dst.at[c], in_sem.at[4 * c + n]))
    load_q = [
        pltpu.make_async_copy(q_hbm.at[c], q_ref.at[c], in_sem.at[8 + c]) for c in range(CONV)
    ]
    load_qf = pltpu.make_async_copy(qf_hbm, qf_ref, in_sem.at[10])
    for load in loads:
        load.start()
    load_qf.start()
    for load in load_q:
        load.start()

    def copy_of(c, send):
        source, part, parts, target, landing = send
        where = pl.ds(part, parts)
        return pltpu.make_async_remote_copy(
            src_ref=held[c].at[SLOT_OF[source], where],
            dst_ref=held[c].at[SLOT_OF[landing], where],
            send_sem=send_sem.at[c, SEND_INDEX[send]],
            recv_sem=recv_sem.at[c, SEND_INDEX[send]],
            device_id={"ctx": devices[target]},
            device_id_type=MESH,
        )

    block = [[order[c, 2 * me + half] for half in range(2)] for c in range(CONV)]
    low_half = [jnp.where(block[c][0] < block[c][1], 0, 1) for c in range(CONV)]
    low_block = [jnp.minimum(block[c][0], block[c][1]) for c in range(CONV)]
    for c in range(CONV):
        for load in loads[4 * c : 4 * c + 4]:
            load.wait()
        for part, (rows, later) in enumerate(((k_ref, kf_ref), (v_ref, vf_ref))):
            first, second = rows[c, 0], rows[c, 1]
            held[c][0, part, 0:HALF, :] = jnp.where(low_half[c] == 0, first, second)
            held[c][0, part, HALF : 2 * HALF, :] = jnp.where(low_half[c] == 0, second, first)
            held[c][0, part, 2 * HALF : CHUNK, :] = later[c]

    def arrive(c, slot):
        for send in ALL_SENDS:
            if send[4] == slot:
                copy_of(c, send).wait_recv()
        for send in FORWARDS.get(slot, ()):
            copy_of(c, send).start()

    step_top[0] = jnp.full((GROUP * HALF, 128), FLOOR, jnp.float32)
    step_total[0] = jnp.zeros((GROUP * HALF, 2 * HEAD_DIM), jnp.float32)

    def iotas(rows):
        return (
            lax.broadcasted_iota(jnp.int32, (rows, 128), 0),
            lax.broadcasted_iota(jnp.int32, (rows, 128), 1),
        )

    row, lane = iotas(HALF)
    unit_mask[0] = jnp.zeros((HALF, 128), jnp.bfloat16)
    unit_mask[1] = jnp.where(lane == row, 1.0, 0.0).astype(jnp.bfloat16)
    unit_mask[2] = jnp.where(lane == HALF, 1.0, 0.0).astype(jnp.bfloat16)
    hidden = jnp.where(((lane > row) & (lane < HALF)) | (lane == HALF), HIDE, 0.0).astype(jnp.bfloat16)
    for h in range(PROMPT_HEADS):
        p_query_mask[h * HALF : (h + 1) * HALF, :] = hidden
    row, lane = iotas(FOLLOW)
    hidden = jnp.where(((lane > row) & (lane < FOLLOW)) | (lane == FOLLOW), HIDE, 0.0).astype(jnp.bfloat16)
    for h in range(FOLLOW_HEADS):
        f_query_mask[h * FOLLOW : (h + 1) * FOLLOW, :] = hidden
    for c in range(CONV):
        for slot, offset in enumerate(SLOTS):
            owner = devices[offset]
            lower = jnp.minimum(order[c, 2 * owner], order[c, 2 * owner + 1])
            row, lane = iotas(HALF)
            for half, number in enumerate((lower, 31 - lower)):
                dead = (row + number * HALF >= lengths[c, 0]) & (lane == FOLLOW)
                f_mask[c, slot, half * HALF : (half + 1) * HALF, :] = jnp.where(dead, 1.0, 0.0).astype(
                    jnp.bfloat16
                )
            row, lane = iotas(FOLLOW)
            position = row + owner * FOLLOW
            if slot == 0:
                seen = (lane == row) | ((position >= lengths[c, 1]) & (lane == FOLLOW))
            else:
                last = jnp.minimum(lengths[c, 1], me * FOLLOW)
                seen = (position >= last) & (lane == FOLLOW)
            f_mask[c, slot, 2 * HALF : CHUNK, :] = jnp.where(seen, 1.0, 0.0).astype(jnp.bfloat16)

    pl.semaphore_wait(barrier, len(OWN_SENDS))
    for c in range(CONV):
        for send in OWN_SENDS:
            copy_of(c, send).start()

    def place(c, number):
        found = jnp.int32(0)
        for slot, offset in enumerate(SLOTS):
            owner = devices[offset]
            lower = jnp.minimum(order[c, 2 * owner], order[c, 2 * owner + 1])
            found = jnp.where(lower == number, slot, found)
        return found

    def prompt_query(c, half, tile):
        start = tile * (PROMPT_HEADS * HEAD_DIM)
        return jnp.concatenate(
            [
                q_ref[c, half, :, start + h * HEAD_DIM : start + (h + 1) * HEAD_DIM]
                for h in range(PROMPT_HEADS)
            ],
            axis=0,
        )

    def state(tops, totals, rows, first):
        def before():
            return (None, None) if first else (tops[rows, :], totals[rows, :])

        def after(top, total):
            tops[rows, :] = top
            totals[rows, :] = total

        return before, after

    def high_on_low(c, slots, first):
        units = []
        for tile in range(GROUP // PROMPT_HEADS):
            rows = pl.ds(tile * PROMPT_TILE, PROMPT_TILE)
            units.append(
                (
                    functools.partial(prompt_query, c, 1 - low_half[c], tile),
                    lambda: jnp.concatenate([held[c][s, 0, 0:HALF, :] for s in slots], axis=0),
                    lambda: jnp.concatenate([held[c][s, 1, 0:HALF, :] for s in slots], axis=0),
                )
                + state(step_top.at[1 + c], step_total.at[1 + c], rows, first)
            )
        return units

    def follow(c, slots, first):
        units = []
        for tile in range(GROUP // FOLLOW_HEADS):
            rows = pl.ds(tile * FOLLOW_TILE, FOLLOW_TILE)

            def query(start=tile * FOLLOW_HEADS * HEAD_DIM):
                heads = [
                    qf_ref[c, :, start + h * HEAD_DIM : start + (h + 1) * HEAD_DIM]
                    for h in range(FOLLOW_HEADS)
                ]
                return jnp.concatenate([jnp.concatenate(heads, axis=0), f_query_mask[...]], axis=1)

            units.append(
                (
                    query,
                    lambda: jnp.concatenate(
                        [jnp.concatenate([held[c][s, 0], f_mask[c, s]], axis=1) for s in slots],
                        axis=0,
                    ),
                    lambda: jnp.concatenate([held[c][s, 1] for s in slots], axis=0),
                )
                + state(f_top.at[c], f_total.at[c], rows, first)
            )
        return units

    stores = []

    def store(src, dst):
        copy = pltpu.make_async_copy(src, dst, out_sem.at[len(stores)])
        copy.start()
        stores.append(copy)

    def finish_follow(c):
        live = lax.broadcasted_iota(jnp.int32, (FOLLOW, HEAD_DIM), 0) + me * FOLLOW < lengths[c, 1]
        for h in range(GROUP):
            rows = pl.ds(h * FOLLOW, FOLLOW)
            result = f_total[c, rows, 0:HEAD_DIM] / f_total[c, rows, HEAD_DIM:]
            outf_ref[c, :, h * HEAD_DIM : (h + 1) * HEAD_DIM] = jnp.where(live, result, 0.0).astype(
                jnp.bfloat16
            )
        store(outf_ref.at[c], outf_hbm.at[c])

    def rest(c):
        mine = low_block[c]
        case = mine // 4

        def pick(*by_case):
            return jnp.where(
                case == 0, by_case[0], jnp.where(case == 1, by_case[1], jnp.where(case == 2, by_case[2], by_case[3]))
            )

        is_high = (pick(1, 0, 0, 0), pick(1, 1, 1, 0), pick(0, 1, 0, 1))
        offset = (0, pick(8, 0, 0, 8), pick(0, 8, 8, 0))
        begun = 1 + c
        before_of = (pick(begun, 0, 0, 0), pick(3, begun, begun, 3), pick(0, 4, 3, begun))
        last_low, last_high = pick(5, 3, 5, 4), pick(4, 5, 4, 5)
        units = []
        for t, size in enumerate(REST_TILES):
            blocks = []
            for w in range(size):
                reach = jnp.where(is_high[t] == 1, 15 - mine, mine)
                ahead = reach - (offset[t] + w)
                number = jnp.where(is_high[t] == 1, mine + ahead, mine - ahead)
                number = jnp.minimum(jnp.maximum(number, 0), CTX - 1)
                kind = jnp.where(ahead > 0, 0, jnp.where(ahead == 0, 1, 2))
                blocks.append((place(c, number), kind))
            half = jnp.where(is_high[t] == 1, 1 - low_half[c], low_half[c])

            def rows_of(slot, part, high=is_high[t]):
                return jnp.where(
                    high == 1, held[c][slot, part, HALF : 2 * HALF, :], held[c][slot, part, 0:HALF, :]
                )

            def keys(blocks=blocks, rows_of=rows_of):
                return jnp.concatenate(
                    [
                        jnp.concatenate([rows_of(slot, 0), unit_mask[kind]], axis=1)
                        for slot, kind in blocks
                    ],
                    axis=0,
                )

            def values(blocks=blocks, rows_of=rows_of):
                return jnp.concatenate([rows_of(slot, 1) for slot, _ in blocks], axis=0)

            for tile in range(GROUP // PROMPT_HEADS):
                rows = pl.ds(tile * PROMPT_TILE, PROMPT_TILE)

                def query(half=half, tile=tile):
                    return jnp.concatenate([prompt_query(c, half, tile), p_query_mask[...]], axis=1)

                def before(t=t, rows=rows):
                    return step_top[before_of[t], rows, :], step_total[before_of[t], rows, :]

                def after(top, total, t=t, rows=rows):
                    step_top[t + 3, rows, :] = top
                    step_total[t + 3, rows, :] = total

                units.append((query, keys, values, before, after))

        def finish(tile):
            for half in range(2):
                last = jnp.where(low_half[c] == half, last_low, last_high)
                position = (
                    lax.broadcasted_iota(jnp.int32, (HALF, HEAD_DIM), 0) + block[c][half] * HALF
                )
                live = position < lengths[c, 0]
                for h in range(tile * PROMPT_HEADS, (tile + 1) * PROMPT_HEADS):
                    rows = pl.ds(h * HALF, HALF)
                    result = step_total[last, rows, 0:HEAD_DIM] / step_total[last, rows, HEAD_DIM:]
                    out_ref[c, half, :, h * HEAD_DIM : (h + 1) * HEAD_DIM] = jnp.where(
                        live, result, 0.0
                    ).astype(jnp.bfloat16)
            columns = pl.ds(tile * PROMPT_HEADS * HEAD_DIM, PROMPT_HEADS * HEAD_DIM)
            store(out_ref.at[c, :, :, columns], out_hbm.at[c, :, :, columns])

        finishes = [functools.partial(finish, tile) for tile in range(GROUP // PROMPT_HEADS)]
        return units, finishes

    schedule(arrive, high_on_low, follow, finish_follow, rest, load_q, load_qf)
    for c in range(CONV):
        for send in ALL_SENDS:
            copy_of(c, send).wait_send()
    for copy in stores:
        copy.wait()


def schedule(arrive, high_on_low, follow, finish_follow, rest, load_q, load_qf):
    near = (0, 1, 2, 3, 4, 5, 6, 7)
    middle = (8, 9, 10, 11, 12, 13)
    last = (14, 15)
    far = middle + last

    def wait_for(c, *slots):
        def call():
            for slot in slots:
                arrive(c, slot)

        return call

    first = ((3, 0, 0), (1, 0, 0), (0, 1, 0))
    first_shared = ((0, 0, 1), (3, 0, 1), (1, 0, 1), (0, 1, 1))
    second = ((3, 1, 0), (1, 1, 0))
    middle_shared = ((3, 1, 1), (1, 1, 1), (2, 0, 1))
    load_qf.wait()
    for load in load_q:
        load.wait()
    h, f = high_on_low(0, near, True), follow(0, near, True)
    items = [wait_for(0, *first), wait_for(0, *first_shared)]
    items += h[:2] + [wait_for(1, *first)] + h[2:] + f
    h, f = high_on_low(1, near, True), follow(1, near, True)
    items += [wait_for(1, *first_shared), wait_for(0, (2, 0, 0))]
    items += h[:3] + [wait_for(0, *second)] + h[3:] + [wait_for(1, (2, 0, 0))] + f
    h, f = high_on_low(0, middle, False), follow(0, middle, False)
    items += [wait_for(0, *middle_shared)]
    items += h[:2] + [wait_for(1, *second)] + h[2:] + f[:1] + [wait_for(0, (2, 1, 0))] + f[1:]
    h, f = high_on_low(0, last, False), follow(0, last, False)
    items += [wait_for(0, (2, 1, 1))] + h + f + [wait_for(1, (2, 1, 0))]
    units, finishes = rest(0)
    items += units[:4] + [functools.partial(finish_follow, 0)] + units[4:10] + finishes[:1]
    items += units[10:11] + finishes[1:2] + units[11:]
    h, f = high_on_low(1, far, False), follow(1, far, False)
    items += [wait_for(1, *middle_shared, (2, 1, 1))]
    items += f[:1] + finishes[2:3] + f[1:] + finishes[3:] + h
    units, finishes = rest(1)
    items += units[:4] + [functools.partial(finish_follow, 1)] + units[4:10] + finishes[:1]
    items += units[10:11] + finishes[1:2] + units[11:] + finishes[2:]
    run(items)


def on_device(q_prompt, k_prompt, v_prompt, q_follow, k_follow, v_follow, lengths, block_order):
    width = GROUP * HEAD_DIM
    any_space = pl.BlockSpec(memory_space=pl.ANY)
    smem = pl.BlockSpec(memory_space=pltpu.SMEM)
    bf16, f32 = jnp.bfloat16, jnp.float32
    halves = (CONV, 2, HALF)
    out, out_follow = pl.pallas_call(
        kernel,
        out_shape=(
            jax.ShapeDtypeStruct(halves + (width,), bf16),
            jax.ShapeDtypeStruct((CONV, FOLLOW, width), bf16),
        ),
        in_specs=[smem, smem] + [any_space] * 6,
        out_specs=(any_space, any_space),
        scratch_shapes=[
            pltpu.VMEM(halves + (width,), bf16),
            pltpu.VMEM(halves + (HEAD_DIM,), bf16),
            pltpu.VMEM(halves + (HEAD_DIM,), bf16),
            pltpu.VMEM((CONV, FOLLOW, width), bf16),
            pltpu.VMEM((CONV, FOLLOW, HEAD_DIM), bf16),
            pltpu.VMEM((CONV, FOLLOW, HEAD_DIM), bf16),
            pltpu.VMEM(halves + (width,), bf16),
            pltpu.VMEM((CONV, FOLLOW, width), bf16),
            pltpu.VMEM((CTX, 2, CHUNK, HEAD_DIM), bf16),
            pltpu.VMEM((CTX, 2, CHUNK, HEAD_DIM), bf16),
            pltpu.VMEM((CONV, CTX, CHUNK, HEAD_DIM), bf16),
            pltpu.VMEM((3, HALF, HEAD_DIM), bf16),
            pltpu.VMEM((PROMPT_TILE, HEAD_DIM), bf16),
            pltpu.VMEM((FOLLOW_TILE, HEAD_DIM), bf16),
            pltpu.VMEM((1 + CONV + len(REST_TILES), GROUP * HALF, HEAD_DIM), f32),
            pltpu.VMEM((1 + CONV + len(REST_TILES), GROUP * HALF, 2 * HEAD_DIM), f32),
            pltpu.VMEM((CONV, GROUP * FOLLOW, HEAD_DIM), f32),
            pltpu.VMEM((CONV, GROUP * FOLLOW, 2 * HEAD_DIM), f32),
            pltpu.SemaphoreType.DMA((11,)),
            pltpu.SemaphoreType.DMA((CONV + CONV * (GROUP // PROMPT_HEADS),)),
            pltpu.SemaphoreType.DMA((CONV, len(ALL_SENDS))),
            pltpu.SemaphoreType.DMA((CONV, len(ALL_SENDS))),
        ],
        compiler_params=pltpu.CompilerParams(
            collective_id=0, has_side_effects=True, vmem_limit_bytes=63 << 20
        ),
        cost_estimate=pl.CostEstimate(
            flops=7_400_000_000, bytes_accessed=8_000_000, transcendentals=15_000_000
        ),
    )(
        lengths,
        block_order,
        q_prompt.reshape(halves + (width,)),
        k_prompt.reshape(halves + (HEAD_DIM,)),
        v_prompt.reshape(halves + (HEAD_DIM,)),
        q_follow,
        k_follow,
        v_follow,
    )
    return out.reshape(q_prompt.shape), out_follow


def solution(mesh):
    return jax.shard_map(
        on_device,
        mesh=mesh,
        in_specs=(P("dp", "ctx", "tp"),) * 6 + (P("dp", None), P("dp", None)),
        out_specs=(P("dp", "ctx", "tp"), P("dp", "ctx", "tp")),
        check_vma=False,
    )
```

```python
import functools
import math

import jax
import jax.numpy as jnp
from jax import lax
from jax.experimental import pallas as pl
from jax.experimental.pallas import tpu as pltpu
from jax.sharding import PartitionSpec as P

HEAD_DIM = 128
CONV = 2
HALF = 96
FOLLOW = 32
CHUNK = 2 * HALF + FOLLOW
GROUP = 16
CTX = 16
PROMPT_TILE = 384
PROMPT_HEADS = PROMPT_TILE // HALF
FOLLOW_TILE = 256
FOLLOW_HEADS = FOLLOW_TILE // FOLLOW
REST_TILES = (8, 8, 4)
HIDE = -1e30
FLOOR = -1e20
SCALE = math.log2(math.e) / math.sqrt(HEAD_DIM)
MESH = pl.DeviceIdType.MESH

CHIPS = ((0, 0), (3, 0), (1, 0), (0, 1), (3, 1), (1, 1), (2, 0), (2, 1))
PLACES = tuple(chip + (dk,) for dk in range(2) for chip in CHIPS)
SHARED = len(CHIPS)
RIGHT, LEFT, ACROSS, BESIDE = (1, 0, 0), (3, 0, 0), (0, 1, 0), (0, 0, 1)

SENDS = {
    "own": (
        (0, 1, 0, 2, RIGHT, 1),
        (0, 1, 0, 2, LEFT, 2),
        (0, 1, 0, 2, ACROSS, 3),
        (0, 1, 0, 2, BESIDE, SHARED),
    ),
    "first": (
        (3, 1, 0, 2, RIGHT, 4),
        (3, 1, 0, 2, LEFT, 5),
        (1, 1, 0, 1, RIGHT, 6),
        (2, 1, 1, 1, LEFT, 6),
        (1, 3, 0, 2, BESIDE, SHARED + 1),
    ),
    "second": (
        (4, 1, 0, 1, RIGHT, 7),
        (5, 1, 1, 1, LEFT, 7),
        (4, 3, 0, 2, BESIDE, SHARED + 4),
    ),
    "third": ((7, 1, 0, 2, BESIDE, SHARED + 7),),
}
ALL_SENDS = tuple(send for sends in SENDS.values() for send in sends)
SEND_INDEX = {send: n for n, send in enumerate(ALL_SENDS)}


def scores_of(query, keys):
    return lax.dot_general(
        query, keys, (((1,), (1,)), ((), ())), preferred_element_type=jnp.float32
    )


def weigh(scores, highest):
    top = jnp.maximum(jnp.max(scores, axis=1, keepdims=True), FLOOR)
    if highest is None:
        top = jnp.broadcast_to(top, (scores.shape[0], 128))
        factor = None
    else:
        top = jnp.maximum(highest, top)
        factor = jnp.exp2((highest - top) * SCALE)
    width = scores.shape[1]
    spread = jnp.tile(top, (1, -(-width // 128)))[:, :width]
    return top, jnp.exp2((scores - spread) * SCALE).astype(jnp.bfloat16), factor


def run(items):
    steps, calls = [], [[]]
    for item in items:
        if callable(item):
            calls[-1].append(item)
        else:
            steps.append(item)
            calls.append([])

    def begin(n):
        for call in calls[n]:
            call()
        return scores_of(steps[n][0](), steps[n][1]())

    ahead = begin(0)
    for n, (_, _, values, before, after) in enumerate(steps):
        scores = ahead
        if n + 1 < len(steps):
            ahead = begin(n + 1)
        highest, total = before()
        top, weights, factor = weigh(scores, highest)
        rows = values()
        added = jnp.dot(
            weights,
            jnp.concatenate([rows, jnp.ones_like(rows)], axis=1),
            preferred_element_type=jnp.float32,
        )
        if total is not None:
            added = added + total * jnp.tile(factor, (1, 2))
        after(top, added)
    for call in calls[-1]:
        call()


def kernel(
    lengths, order, q_hbm, k_hbm, v_hbm, qf_hbm, kf_hbm, vf_hbm,
    out_ref, outf_ref,
    q_ref, k_ref, v_ref, qf_ref, kf_ref, vf_ref,
    held0, held1, f_mask, unit_mask, p_query_mask, f_query_mask,
    step_top, step_total, f_top, f_total,
    in_sem, send_sem, recv_sem,
):
    held = (held0, held1)
    me = lax.axis_index("ctx")
    my_x, my_y, my_k = me // 4, lax.rem(me // 2, 2), lax.rem(me, 2)

    devices = {
        (dx, dy, dk): (lax.rem(my_x + dx, 4) * 2 + lax.rem(my_y + dy, 2)) * 2 + lax.rem(my_k + dk, 2)
        for dx, dy, dk in PLACES
    }

    barrier = pltpu.get_barrier_semaphore()
    for send in SENDS["own"]:
        pl.semaphore_signal(barrier, inc=1, device_id={"ctx": devices[send[4]]}, device_id_type=MESH)

    loads = []
    for c in range(CONV):
        for n, (src, dst) in enumerate(
            ((k_hbm, k_ref), (v_hbm, v_ref), (kf_hbm, kf_ref), (vf_hbm, vf_ref))
        ):
            loads.append(pltpu.make_async_copy(src.at[c], dst.at[c], in_sem.at[4 * c + n]))
    load_q = [
        pltpu.make_async_copy(q_hbm.at[c], q_ref.at[c], in_sem.at[8 + c]) for c in range(CONV)
    ]
    load_qf = pltpu.make_async_copy(qf_hbm, qf_ref, in_sem.at[10])
    for load in loads:
        load.start()
    load_qf.start()
    for load in load_q:
        load.start()

    def copy_of(c, send):
        source, slots, part, parts, target, landing = send
        return pltpu.make_async_remote_copy(
            src_ref=held[c].at[pl.ds(source, slots), pl.ds(part, parts)],
            dst_ref=held[c].at[pl.ds(landing, slots), pl.ds(part, parts)],
            send_sem=send_sem.at[c, SEND_INDEX[send]],
            recv_sem=recv_sem.at[c, SEND_INDEX[send]],
            device_id={"ctx": devices[target]},
            device_id_type=MESH,
        )

    block = [[order[c, 2 * me + half] for half in range(2)] for c in range(CONV)]
    low_half = [jnp.where(block[c][0] < block[c][1], 0, 1) for c in range(CONV)]
    low_block = [jnp.minimum(block[c][0], block[c][1]) for c in range(CONV)]
    for c in range(CONV):
        for load in loads[4 * c : 4 * c + 4]:
            load.wait()
        for part, (rows, later) in enumerate(((k_ref, kf_ref), (v_ref, vf_ref))):
            first, second = rows[c, 0], rows[c, 1]
            held[c][0, part, 0:HALF, :] = jnp.where(low_half[c] == 0, first, second)
            held[c][0, part, HALF : 2 * HALF, :] = jnp.where(low_half[c] == 0, second, first)
            held[c][0, part, 2 * HALF : CHUNK, :] = later[c]

    def arrive(c, wave, shared):
        for send in SENDS[wave]:
            if (send[4] == BESIDE) == shared:
                copy_of(c, send).wait_recv()

    def forward(c, wave):
        for send in SENDS[wave]:
            copy_of(c, send).start()

    step_top[0] = jnp.full((GROUP * HALF, 128), FLOOR, jnp.float32)
    step_total[0] = jnp.zeros((GROUP * HALF, 2 * HEAD_DIM), jnp.float32)

    def iotas(rows):
        return (
            lax.broadcasted_iota(jnp.int32, (rows, 128), 0),
            lax.broadcasted_iota(jnp.int32, (rows, 128), 1),
        )

    row, lane = iotas(HALF)
    unit_mask[0] = jnp.zeros((HALF, 128), jnp.bfloat16)
    unit_mask[1] = jnp.where(lane == row, 1.0, 0.0).astype(jnp.bfloat16)
    unit_mask[2] = jnp.where(lane == HALF, 1.0, 0.0).astype(jnp.bfloat16)
    hidden = jnp.where(((lane > row) & (lane < HALF)) | (lane == HALF), HIDE, 0.0).astype(jnp.bfloat16)
    for h in range(PROMPT_HEADS):
        p_query_mask[h * HALF : (h + 1) * HALF, :] = hidden
    row, lane = iotas(FOLLOW)
    hidden = jnp.where(((lane > row) & (lane < FOLLOW)) | (lane == FOLLOW), HIDE, 0.0).astype(jnp.bfloat16)
    for h in range(FOLLOW_HEADS):
        f_query_mask[h * FOLLOW : (h + 1) * FOLLOW, :] = hidden
    for c in range(CONV):
        for slot, offset in enumerate(PLACES):
            owner = devices[offset]
            lower = jnp.minimum(order[c, 2 * owner], order[c, 2 * owner + 1])
            row, lane = iotas(HALF)
            for half, number in enumerate((lower, 31 - lower)):
                dead = (row + number * HALF >= lengths[c, 0]) & (lane == FOLLOW)
                f_mask[c, slot, half * HALF : (half + 1) * HALF, :] = jnp.where(dead, 1.0, 0.0).astype(
                    jnp.bfloat16
                )
            row, lane = iotas(FOLLOW)
            position = row + owner * FOLLOW
            if slot == 0:
                seen = (lane == row) | ((position >= lengths[c, 1]) & (lane == FOLLOW))
            else:
                last = jnp.minimum(lengths[c, 1], me * FOLLOW)
                seen = (position >= last) & (lane == FOLLOW)
            f_mask[c, slot, 2 * HALF : CHUNK, :] = jnp.where(seen, 1.0, 0.0).astype(jnp.bfloat16)

    pl.semaphore_wait(barrier, len(SENDS["own"]))
    for c in range(CONV):
        forward(c, "own")

    def place(c, number):
        found = jnp.int32(0)
        for slot, offset in enumerate(PLACES):
            owner = devices[offset]
            lower = jnp.minimum(order[c, 2 * owner], order[c, 2 * owner + 1])
            found = jnp.where(lower == number, slot, found)
        return found

    def prompt_query(c, half, tile):
        start = tile * (PROMPT_HEADS * HEAD_DIM)
        return jnp.concatenate(
            [
                q_ref[c, half, :, start + h * HEAD_DIM : start + (h + 1) * HEAD_DIM]
                for h in range(PROMPT_HEADS)
            ],
            axis=0,
        )

    def state(tops, totals, rows, first):
        def before():
            return (None, None) if first else (tops[rows, :], totals[rows, :])

        def after(top, total):
            tops[rows, :] = top
            totals[rows, :] = total

        return before, after

    def high_on_low(c, slots, first):
        units = []
        for tile in range(GROUP // PROMPT_HEADS):
            rows = pl.ds(tile * PROMPT_TILE, PROMPT_TILE)
            units.append(
                (
                    functools.partial(prompt_query, c, 1 - low_half[c], tile),
                    lambda: jnp.concatenate([held[c][s, 0, 0:HALF, :] for s in slots], axis=0),
                    lambda: jnp.concatenate([held[c][s, 1, 0:HALF, :] for s in slots], axis=0),
                )
                + state(step_top.at[1 + c], step_total.at[1 + c], rows, first)
            )
        return units

    def follow(c, slots, first):
        units = []
        for tile in range(GROUP // FOLLOW_HEADS):
            rows = pl.ds(tile * FOLLOW_TILE, FOLLOW_TILE)

            def query(start=tile * FOLLOW_HEADS * HEAD_DIM):
                heads = [
                    qf_ref[c, :, start + h * HEAD_DIM : start + (h + 1) * HEAD_DIM]
                    for h in range(FOLLOW_HEADS)
                ]
                return jnp.concatenate([jnp.concatenate(heads, axis=0), f_query_mask[...]], axis=1)

            units.append(
                (
                    query,
                    lambda: jnp.concatenate(
                        [jnp.concatenate([held[c][s, 0], f_mask[c, s]], axis=1) for s in slots],
                        axis=0,
                    ),
                    lambda: jnp.concatenate([held[c][s, 1] for s in slots], axis=0),
                )
                + state(f_top.at[c], f_total.at[c], rows, first)
            )
        return units

    def finish_follow(c):
        live = lax.broadcasted_iota(jnp.int32, (FOLLOW, HEAD_DIM), 0) + me * FOLLOW < lengths[c, 1]
        for h in range(GROUP):
            rows = pl.ds(h * FOLLOW, FOLLOW)
            result = f_total[c, rows, 0:HEAD_DIM] / f_total[c, rows, HEAD_DIM:]
            outf_ref[c, :, h * HEAD_DIM : (h + 1) * HEAD_DIM] = jnp.where(live, result, 0.0).astype(
                jnp.bfloat16
            )
    def rest(c):
        mine = low_block[c]
        case = mine // 4

        def pick(*by_case):
            return jnp.where(
                case == 0, by_case[0], jnp.where(case == 1, by_case[1], jnp.where(case == 2, by_case[2], by_case[3]))
            )

        is_high = (pick(1, 0, 0, 0), pick(1, 1, 1, 0), pick(0, 1, 0, 1))
        offset = (0, pick(8, 0, 0, 8), pick(0, 8, 8, 0))
        begun = 1 + c
        before_of = (pick(begun, 0, 0, 0), pick(3, begun, begun, 3), pick(0, 4, 3, begun))
        last_low, last_high = pick(5, 3, 5, 4), pick(4, 5, 4, 5)
        units = []
        for t, size in enumerate(REST_TILES):
            blocks = []
            for w in range(size):
                reach = jnp.where(is_high[t] == 1, 15 - mine, mine)
                ahead = reach - (offset[t] + w)
                number = jnp.where(is_high[t] == 1, mine + ahead, mine - ahead)
                number = jnp.minimum(jnp.maximum(number, 0), CTX - 1)
                kind = jnp.where(ahead > 0, 0, jnp.where(ahead == 0, 1, 2))
                blocks.append((place(c, number), kind))
            half = jnp.where(is_high[t] == 1, 1 - low_half[c], low_half[c])

            def rows_of(slot, part, high=is_high[t]):
                return jnp.where(
                    high == 1, held[c][slot, part, HALF : 2 * HALF, :], held[c][slot, part, 0:HALF, :]
                )

            def keys(blocks=blocks, rows_of=rows_of):
                return jnp.concatenate(
                    [
                        jnp.concatenate([rows_of(slot, 0), unit_mask[kind]], axis=1)
                        for slot, kind in blocks
                    ],
                    axis=0,
                )

            def values(blocks=blocks, rows_of=rows_of):
                return jnp.concatenate([rows_of(slot, 1) for slot, _ in blocks], axis=0)

            for tile in range(GROUP // PROMPT_HEADS):
                rows = pl.ds(tile * PROMPT_TILE, PROMPT_TILE)

                def query(half=half, tile=tile):
                    return jnp.concatenate([prompt_query(c, half, tile), p_query_mask[...]], axis=1)

                def before(t=t, rows=rows):
                    return step_top[before_of[t], rows, :], step_total[before_of[t], rows, :]

                def after(top, total, t=t, rows=rows):
                    step_top[t + 3, rows, :] = top
                    step_total[t + 3, rows, :] = total

                units.append((query, keys, values, before, after))

        def finish(tile):
            for half in range(2):
                last = jnp.where(low_half[c] == half, last_low, last_high)
                position = (
                    lax.broadcasted_iota(jnp.int32, (HALF, HEAD_DIM), 0) + block[c][half] * HALF
                )
                live = position < lengths[c, 0]
                for h in range(tile * PROMPT_HEADS, (tile + 1) * PROMPT_HEADS):
                    rows = pl.ds(h * HALF, HALF)
                    result = step_total[last, rows, 0:HEAD_DIM] / step_total[last, rows, HEAD_DIM:]
                    out_ref[c, half, :, h * HEAD_DIM : (h + 1) * HEAD_DIM] = jnp.where(
                        live, result, 0.0
                    ).astype(jnp.bfloat16)

        finishes = [functools.partial(finish, tile) for tile in range(GROUP // PROMPT_HEADS)]
        return units, finishes

    schedule(arrive, forward, high_on_low, follow, finish_follow, rest, load_q, load_qf)
    for c in range(CONV):
        for send in ALL_SENDS:
            copy_of(c, send).wait_send()


def schedule(arrive, forward, high_on_low, follow, finish_follow, rest, load_q, load_qf):
    near = (0, 1, 2, 3, 8, 9, 10, 11)
    middle = (4, 5, 6, 12, 13, 14)
    last = (7, 15)
    far = middle + last
    following = {"own": "first", "first": "second", "second": "third"}

    def chips(c, wave):
        def call():
            arrive(c, wave, False)
            forward(c, following[wave])

        return call

    def cores(c, *waves):
        def call():
            for wave in waves:
                arrive(c, wave, True)

        return call

    load_qf.wait()
    for load in load_q:
        load.wait()
    h, f = high_on_low(0, near, True), follow(0, near, True)
    items = [chips(0, "own"), cores(0, "own", "first")]
    items += h + [chips(1, "own")] + f
    h, f = high_on_low(1, near, True), follow(1, near, True)
    items += [cores(1, "own", "first")] + h + [chips(0, "first")] + f
    h, f = high_on_low(0, middle, False), follow(0, middle, False)
    items += [cores(0, "second")] + h + [chips(1, "first")] + f[:1] + [chips(0, "second")] + f[1:]
    h, f = high_on_low(0, last, False), follow(0, last, False)
    items += [cores(0, "third")] + h + f
    units, finishes = rest(0)
    items += units[:2] + [chips(1, "second")] + units[2:4]
    items += [functools.partial(finish_follow, 0)] + units[4:10] + finishes[:1]
    items += units[10:11] + finishes[1:2] + units[11:]
    h, f = high_on_low(1, far, False), follow(1, far, False)
    items += [cores(1, "second", "third")]
    items += f[:1] + finishes[2:3] + f[1:] + finishes[3:] + h
    units, finishes = rest(1)
    items += units[:4] + [functools.partial(finish_follow, 1)] + units[4:10] + finishes[:1]
    items += units[10:11] + finishes[1:2] + units[11:] + finishes[2:]
    run(items)


def on_device(q_prompt, k_prompt, v_prompt, q_follow, k_follow, v_follow, lengths, block_order):
    width = GROUP * HEAD_DIM
    any_space = pl.BlockSpec(memory_space=pl.ANY)
    smem = pl.BlockSpec(memory_space=pltpu.SMEM)
    bf16, f32 = jnp.bfloat16, jnp.float32
    halves = (CONV, 2, HALF)
    out, out_follow = pl.pallas_call(
        kernel,
        out_shape=(
            pltpu.VMEM(halves + (width,), bf16),
            pltpu.VMEM((CONV, FOLLOW, width), bf16),
        ),
        in_specs=[smem, smem] + [any_space] * 6,
        out_specs=(pl.BlockSpec(memory_space=pltpu.VMEM),) * 2,
        scratch_shapes=[
            pltpu.VMEM(halves + (width,), bf16),
            pltpu.VMEM(halves + (HEAD_DIM,), bf16),
            pltpu.VMEM(halves + (HEAD_DIM,), bf16),
            pltpu.VMEM((CONV, FOLLOW, width), bf16),
            pltpu.VMEM((CONV, FOLLOW, HEAD_DIM), bf16),
            pltpu.VMEM((CONV, FOLLOW, HEAD_DIM), bf16),
            pltpu.VMEM((CTX, 2, CHUNK, HEAD_DIM), bf16),
            pltpu.VMEM((CTX, 2, CHUNK, HEAD_DIM), bf16),
            pltpu.VMEM((CONV, CTX, CHUNK, HEAD_DIM), bf16),
            pltpu.VMEM((3, HALF, HEAD_DIM), bf16),
            pltpu.VMEM((PROMPT_TILE, HEAD_DIM), bf16),
            pltpu.VMEM((FOLLOW_TILE, HEAD_DIM), bf16),
            pltpu.VMEM((1 + CONV + len(REST_TILES), GROUP * HALF, HEAD_DIM), f32),
            pltpu.VMEM((1 + CONV + len(REST_TILES), GROUP * HALF, 2 * HEAD_DIM), f32),
            pltpu.VMEM((CONV, GROUP * FOLLOW, HEAD_DIM), f32),
            pltpu.VMEM((CONV, GROUP * FOLLOW, 2 * HEAD_DIM), f32),
            pltpu.SemaphoreType.DMA((11,)),
            pltpu.SemaphoreType.DMA((CONV, len(ALL_SENDS))),
            pltpu.SemaphoreType.DMA((CONV, len(ALL_SENDS))),
        ],
        compiler_params=pltpu.CompilerParams(
            collective_id=0, has_side_effects=True, vmem_limit_bytes=61 << 20
        ),
        cost_estimate=pl.CostEstimate(
            flops=7_400_000_000, bytes_accessed=8_000_000, transcendentals=15_000_000
        ),
    )(
        lengths,
        block_order,
        q_prompt.reshape(halves + (width,)),
        k_prompt.reshape(halves + (HEAD_DIM,)),
        v_prompt.reshape(halves + (HEAD_DIM,)),
        q_follow,
        k_follow,
        v_follow,
    )
    return out.reshape(q_prompt.shape), out_follow


def solution(mesh):
    return jax.shard_map(
        on_device,
        mesh=mesh,
        in_specs=(P("dp", "ctx", "tp"),) * 6 + (P("dp", None), P("dp", None)),
        out_specs=(P("dp", "ctx", "tp"), P("dp", "ctx", "tp")),
        check_vma=False,
    )
```

```python
import functools
import math

import jax
import jax.numpy as jnp
from jax import lax
from jax.experimental import pallas as pl
from jax.experimental.pallas import tpu as pltpu
from jax.sharding import PartitionSpec as P

HEAD_DIM = 128
CONV = 2
HALF = 96
FOLLOW = 32
CHUNK = 2 * HALF + FOLLOW
GROUP = 16
CTX = 16
PROMPT_TILE = 384
PROMPT_HEADS = PROMPT_TILE // HALF
FOLLOW_TILE = 256
FOLLOW_HEADS = FOLLOW_TILE // FOLLOW
REST_TILES = (8, 8, 4)
HIDE = -1e30
FLOOR = -1e20
SCALE = math.log2(math.e) / math.sqrt(HEAD_DIM)
MESH = pl.DeviceIdType.MESH

CHIPS = ((0, 0), (3, 0), (1, 0), (0, 1), (3, 1), (1, 1), (2, 0), (2, 1))
PLACES = tuple(chip + (dk,) for dk in range(2) for chip in CHIPS)
SHARED = len(CHIPS)
RIGHT, LEFT, ACROSS, BESIDE = (1, 0, 0), (3, 0, 0), (0, 1, 0), (0, 0, 1)

SENDS = {
    "own": (
        (0, 1, 0, 2, RIGHT, 1),
        (0, 1, 0, 2, LEFT, 2),
        (0, 1, 0, 2, ACROSS, 3),
        (0, 1, 0, 2, BESIDE, SHARED),
    ),
    "first": (
        (3, 1, 0, 2, RIGHT, 4),
        (3, 1, 0, 2, LEFT, 5),
        (1, 1, 0, 1, RIGHT, 6),
        (2, 1, 1, 1, LEFT, 6),
        (1, 3, 0, 2, BESIDE, SHARED + 1),
    ),
    "second": (
        (4, 1, 0, 1, RIGHT, 7),
        (5, 1, 1, 1, LEFT, 7),
        (4, 3, 0, 2, BESIDE, SHARED + 4),
    ),
    "third": ((7, 1, 0, 2, BESIDE, SHARED + 7),),
}
ALL_SENDS = tuple(send for sends in SENDS.values() for send in sends)
SEND_INDEX = {send: n for n, send in enumerate(ALL_SENDS)}


def scores_of(query, keys):
    return lax.dot_general(
        query, keys, (((1,), (1,)), ((), ())), preferred_element_type=jnp.float32
    )


def weigh(scores, highest):
    top = jnp.maximum(jnp.max(scores, axis=1, keepdims=True), FLOOR)
    if highest is None:
        top = jnp.broadcast_to(top, (scores.shape[0], 128))
        factor = None
    else:
        top = jnp.maximum(highest, top)
        factor = jnp.exp2((highest - top) * SCALE)
    width = scores.shape[1]
    spread = jnp.tile(top, (1, -(-width // 128)))[:, :width]
    return top, jnp.exp2((scores - spread) * SCALE).astype(jnp.bfloat16), factor


def run(items):
    steps, calls = [], [[]]
    for item in items:
        if callable(item):
            calls[-1].append(item)
        else:
            steps.append(item)
            calls.append([])

    def begin(n):
        for call in calls[n]:
            call()
        return scores_of(steps[n][0](), steps[n][1]())

    ahead = begin(0)
    for n, (_, _, values, before, after) in enumerate(steps):
        scores = ahead
        if n + 1 < len(steps):
            ahead = begin(n + 1)
        highest, total = before()
        top, weights, factor = weigh(scores, highest)
        rows = values()
        added = jnp.dot(
            weights,
            jnp.concatenate([rows, jnp.ones_like(rows)], axis=1),
            preferred_element_type=jnp.float32,
        )
        if total is not None:
            added = added + total * jnp.tile(factor, (1, 2))
        after(top, added)
    for call in calls[-1]:
        call()


def kernel(
    lengths, order, q_hbm, k_hbm, v_hbm, qf_hbm, kf_hbm, vf_hbm,
    out_ref, outf_ref,
    q_ref, k_ref, v_ref, qf_ref, kf_ref, vf_ref,
    held0, held1, f_mask, unit_mask, p_query_mask, f_query_mask,
    step_top, step_total, f_top, f_total,
    in_sem, send_sem, recv_sem,
):
    held = (held0, held1)
    me = lax.axis_index("ctx")
    my_x, my_y, my_k = me // 4, lax.rem(me // 2, 2), lax.rem(me, 2)

    devices = {
        (dx, dy, dk): (lax.rem(my_x + dx, 4) * 2 + lax.rem(my_y + dy, 2)) * 2 + lax.rem(my_k + dk, 2)
        for dx, dy, dk in PLACES
    }

    barrier = pltpu.get_barrier_semaphore()
    for send in SENDS["own"]:
        pl.semaphore_signal(barrier, inc=1, device_id={"ctx": devices[send[4]]}, device_id_type=MESH)

    loads = []
    for c in range(CONV):
        for n, (src, dst) in enumerate(
            ((k_hbm, k_ref), (v_hbm, v_ref), (kf_hbm, kf_ref), (vf_hbm, vf_ref))
        ):
            loads.append(pltpu.make_async_copy(src.at[c], dst.at[c], in_sem.at[4 * c + n]))
    load_q = [
        pltpu.make_async_copy(q_hbm.at[c], q_ref.at[c], in_sem.at[8 + c]) for c in range(CONV)
    ]
    load_qf = pltpu.make_async_copy(qf_hbm, qf_ref, in_sem.at[10])
    for load in loads:
        load.start()
    load_qf.start()
    for load in load_q:
        load.start()

    def copy_of(c, send):
        source, slots, part, parts, target, landing = send
        return pltpu.make_async_remote_copy(
            src_ref=held[c].at[pl.ds(source, slots), pl.ds(part, parts)],
            dst_ref=held[c].at[pl.ds(landing, slots), pl.ds(part, parts)],
            send_sem=send_sem.at[c, SEND_INDEX[send]],
            recv_sem=recv_sem.at[c, SEND_INDEX[send]],
            device_id={"ctx": devices[target]},
            device_id_type=MESH,
        )

    block = [[order[c, 2 * me + half] for half in range(2)] for c in range(CONV)]
    low_half = [jnp.where(block[c][0] < block[c][1], 0, 1) for c in range(CONV)]
    low_block = [jnp.minimum(block[c][0], block[c][1]) for c in range(CONV)]
    for c in range(CONV):
        for load in loads[4 * c : 4 * c + 4]:
            load.wait()
        for part, (rows, later) in enumerate(((k_ref, kf_ref), (v_ref, vf_ref))):
            first, second = rows[c, 0], rows[c, 1]
            held[c][0, part, 0:HALF, :] = jnp.where(low_half[c] == 0, first, second)
            held[c][0, part, HALF : 2 * HALF, :] = jnp.where(low_half[c] == 0, second, first)
            held[c][0, part, 2 * HALF : CHUNK, :] = later[c]

    def arrive(c, wave, shared):
        for send in SENDS[wave]:
            if (send[4] == BESIDE) == shared:
                copy_of(c, send).wait_recv()

    def forward(c, wave):
        for send in SENDS[wave]:
            copy_of(c, send).start()

    pl.semaphore_wait(barrier, len(SENDS["own"]))
    for c in range(CONV):
        forward(c, "own")

    step_top[0] = jnp.full((GROUP * HALF, 128), FLOOR, jnp.float32)
    step_total[0] = jnp.zeros((GROUP * HALF, 2 * HEAD_DIM), jnp.float32)

    def iotas(rows):
        return (
            lax.broadcasted_iota(jnp.int32, (rows, 128), 0),
            lax.broadcasted_iota(jnp.int32, (rows, 128), 1),
        )

    row, lane = iotas(HALF)
    unit_mask[0] = jnp.zeros((HALF, 128), jnp.bfloat16)
    unit_mask[1] = jnp.where(lane == row, 1.0, 0.0).astype(jnp.bfloat16)
    unit_mask[2] = jnp.where(lane == HALF, 1.0, 0.0).astype(jnp.bfloat16)
    hidden = jnp.where(((lane > row) & (lane < HALF)) | (lane == HALF), HIDE, 0.0).astype(jnp.bfloat16)
    for h in range(PROMPT_HEADS):
        p_query_mask[h * HALF : (h + 1) * HALF, :] = hidden
    row, lane = iotas(FOLLOW)
    hidden = jnp.where(((lane > row) & (lane < FOLLOW)) | (lane == FOLLOW), HIDE, 0.0).astype(jnp.bfloat16)
    for h in range(FOLLOW_HEADS):
        f_query_mask[h * FOLLOW : (h + 1) * FOLLOW, :] = hidden
    for c in range(CONV):
        for slot, offset in enumerate(PLACES):
            owner = devices[offset]
            lower = jnp.minimum(order[c, 2 * owner], order[c, 2 * owner + 1])
            row, lane = iotas(HALF)
            for half, number in enumerate((lower, 31 - lower)):
                dead = (row + number * HALF >= lengths[c, 0]) & (lane == FOLLOW)
                f_mask[c, slot, half * HALF : (half + 1) * HALF, :] = jnp.where(dead, 1.0, 0.0).astype(
                    jnp.bfloat16
                )
            row, lane = iotas(FOLLOW)
            position = row + owner * FOLLOW
            if slot == 0:
                seen = (lane == row) | ((position >= lengths[c, 1]) & (lane == FOLLOW))
            else:
                last = jnp.minimum(lengths[c, 1], me * FOLLOW)
                seen = (position >= last) & (lane == FOLLOW)
            f_mask[c, slot, 2 * HALF : CHUNK, :] = jnp.where(seen, 1.0, 0.0).astype(jnp.bfloat16)

    def place(c, number):
        found = jnp.int32(0)
        for slot, offset in enumerate(PLACES):
            owner = devices[offset]
            lower = jnp.minimum(order[c, 2 * owner], order[c, 2 * owner + 1])
            found = jnp.where(lower == number, slot, found)
        return found

    def prompt_query(c, half, tile):
        start = tile * (PROMPT_HEADS * HEAD_DIM)
        return jnp.concatenate(
            [
                q_ref[c, half, :, start + h * HEAD_DIM : start + (h + 1) * HEAD_DIM]
                for h in range(PROMPT_HEADS)
            ],
            axis=0,
        )

    def state(tops, totals, rows, first):
        def before():
            return (None, None) if first else (tops[rows, :], totals[rows, :])

        def after(top, total):
            tops[rows, :] = top
            totals[rows, :] = total

        return before, after

    def high_on_low(c, slots, first):
        units = []
        for tile in range(GROUP // PROMPT_HEADS):
            rows = pl.ds(tile * PROMPT_TILE, PROMPT_TILE)
            units.append(
                (
                    functools.partial(prompt_query, c, 1 - low_half[c], tile),
                    lambda: jnp.concatenate([held[c][s, 0, 0:HALF, :] for s in slots], axis=0),
                    lambda: jnp.concatenate([held[c][s, 1, 0:HALF, :] for s in slots], axis=0),
                )
                + state(step_top.at[1 + c], step_total.at[1 + c], rows, first)
            )
        return units

    def follow(c, slots, first):
        units = []
        for tile in range(GROUP // FOLLOW_HEADS):
            rows = pl.ds(tile * FOLLOW_TILE, FOLLOW_TILE)

            def query(start=tile * FOLLOW_HEADS * HEAD_DIM):
                heads = [
                    qf_ref[c, :, start + h * HEAD_DIM : start + (h + 1) * HEAD_DIM]
                    for h in range(FOLLOW_HEADS)
                ]
                return jnp.concatenate([jnp.concatenate(heads, axis=0), f_query_mask[...]], axis=1)

            units.append(
                (
                    query,
                    lambda: jnp.concatenate(
                        [jnp.concatenate([held[c][s, 0], f_mask[c, s]], axis=1) for s in slots],
                        axis=0,
                    ),
                    lambda: jnp.concatenate([held[c][s, 1] for s in slots], axis=0),
                )
                + state(f_top.at[c], f_total.at[c], rows, first)
            )
        return units

    def finish_follow(c):
        live = lax.broadcasted_iota(jnp.int32, (FOLLOW, HEAD_DIM), 0) + me * FOLLOW < lengths[c, 1]
        for h in range(GROUP):
            rows = pl.ds(h * FOLLOW, FOLLOW)
            result = f_total[c, rows, 0:HEAD_DIM] / f_total[c, rows, HEAD_DIM:]
            outf_ref[c, :, h * HEAD_DIM : (h + 1) * HEAD_DIM] = jnp.where(live, result, 0.0).astype(
                jnp.bfloat16
            )
    def rest(c):
        mine = low_block[c]
        case = mine // 4

        def pick(*by_case):
            return jnp.where(
                case == 0, by_case[0], jnp.where(case == 1, by_case[1], jnp.where(case == 2, by_case[2], by_case[3]))
            )

        is_high = (pick(1, 0, 0, 0), pick(1, 1, 1, 0), pick(0, 1, 0, 1))
        offset = (0, pick(8, 0, 0, 8), pick(0, 8, 8, 0))
        begun = 1 + c
        before_of = (pick(begun, 0, 0, 0), pick(3, begun, begun, 3), pick(0, 4, 3, begun))
        last_low, last_high = pick(5, 3, 5, 4), pick(4, 5, 4, 5)
        units = []
        for t, size in enumerate(REST_TILES):
            blocks = []
            for w in range(size):
                reach = jnp.where(is_high[t] == 1, 15 - mine, mine)
                ahead = reach - (offset[t] + w)
                number = jnp.where(is_high[t] == 1, mine + ahead, mine - ahead)
                number = jnp.minimum(jnp.maximum(number, 0), CTX - 1)
                kind = jnp.where(ahead > 0, 0, jnp.where(ahead == 0, 1, 2))
                blocks.append((place(c, number), kind))
            half = jnp.where(is_high[t] == 1, 1 - low_half[c], low_half[c])

            def rows_of(slot, part, high=is_high[t]):
                return jnp.where(
                    high == 1, held[c][slot, part, HALF : 2 * HALF, :], held[c][slot, part, 0:HALF, :]
                )

            def keys(blocks=blocks, rows_of=rows_of):
                return jnp.concatenate(
                    [
                        jnp.concatenate([rows_of(slot, 0), unit_mask[kind]], axis=1)
                        for slot, kind in blocks
                    ],
                    axis=0,
                )

            def values(blocks=blocks, rows_of=rows_of):
                return jnp.concatenate([rows_of(slot, 1) for slot, _ in blocks], axis=0)

            for tile in range(GROUP // PROMPT_HEADS):
                rows = pl.ds(tile * PROMPT_TILE, PROMPT_TILE)

                def query(half=half, tile=tile):
                    return jnp.concatenate([prompt_query(c, half, tile), p_query_mask[...]], axis=1)

                def before(t=t, rows=rows):
                    return step_top[before_of[t], rows, :], step_total[before_of[t], rows, :]

                def after(top, total, t=t, rows=rows):
                    step_top[t + 3, rows, :] = top
                    step_total[t + 3, rows, :] = total

                units.append((query, keys, values, before, after))

        def finish(tile):
            for half in range(2):
                last = jnp.where(low_half[c] == half, last_low, last_high)
                position = (
                    lax.broadcasted_iota(jnp.int32, (HALF, HEAD_DIM), 0) + block[c][half] * HALF
                )
                live = position < lengths[c, 0]
                for h in range(tile * PROMPT_HEADS, (tile + 1) * PROMPT_HEADS):
                    rows = pl.ds(h * HALF, HALF)
                    result = step_total[last, rows, 0:HEAD_DIM] / step_total[last, rows, HEAD_DIM:]
                    out_ref[c, half, :, h * HEAD_DIM : (h + 1) * HEAD_DIM] = jnp.where(
                        live, result, 0.0
                    ).astype(jnp.bfloat16)

        finishes = [functools.partial(finish, tile) for tile in range(GROUP // PROMPT_HEADS)]
        return units, finishes

    schedule(arrive, forward, high_on_low, follow, finish_follow, rest, load_q, load_qf)
    for c in range(CONV):
        for send in ALL_SENDS:
            copy_of(c, send).wait_send()


def schedule(arrive, forward, high_on_low, follow, finish_follow, rest, load_q, load_qf):
    near = (0, 1, 2, 3, 8, 9, 10, 11)
    middle = (4, 5, 6, 12, 13, 14)
    last = (7, 15)
    far = middle + last
    following = {"own": "first", "first": "second", "second": "third"}

    def chips(c, wave):
        def call():
            arrive(c, wave, False)
            forward(c, following[wave])

        return call

    def cores(c, *waves):
        def call():
            for wave in waves:
                arrive(c, wave, True)

        return call

    load_qf.wait()
    for load in load_q:
        load.wait()
    items = [chips(0, "own")] + follow(0, near[:4], True) + [cores(0, "own", "first")]
    items += high_on_low(0, near, True) + [chips(1, "own")] + follow(0, near[4:], False)
    h, f = high_on_low(1, near, True), follow(1, near, True)
    items += [cores(1, "own", "first")] + h + [chips(0, "first")] + f
    h, f = high_on_low(0, middle, False), follow(0, middle, False)
    items += [cores(0, "second")] + h + f[:1] + [chips(1, "first"), chips(0, "second")] + f[1:]
    h, f = high_on_low(0, last, False), follow(0, last, False)
    items += [cores(0, "third")] + h + f
    units, finishes = rest(0)
    items += units[:2] + [chips(1, "second")] + units[2:4]
    items += [functools.partial(finish_follow, 0)] + units[4:10] + finishes[:1]
    items += units[10:11] + finishes[1:2] + units[11:]
    h, f = high_on_low(1, far, False), follow(1, far, False)
    items += [cores(1, "second", "third")]
    items += f[:1] + finishes[2:3] + f[1:] + finishes[3:] + h
    units, finishes = rest(1)
    items += units[:4] + [functools.partial(finish_follow, 1)] + units[4:10] + finishes[:1]
    items += units[10:11] + finishes[1:2] + units[11:] + finishes[2:]
    run(items)


def on_device(q_prompt, k_prompt, v_prompt, q_follow, k_follow, v_follow, lengths, block_order):
    width = GROUP * HEAD_DIM
    any_space = pl.BlockSpec(memory_space=pl.ANY)
    smem = pl.BlockSpec(memory_space=pltpu.SMEM)
    bf16, f32 = jnp.bfloat16, jnp.float32
    halves = (CONV, 2, HALF)
    out, out_follow = pl.pallas_call(
        kernel,
        out_shape=(
            pltpu.VMEM(halves + (width,), bf16),
            pltpu.VMEM((CONV, FOLLOW, width), bf16),
        ),
        in_specs=[smem, smem] + [any_space] * 6,
        out_specs=(pl.BlockSpec(memory_space=pltpu.VMEM),) * 2,
        scratch_shapes=[
            pltpu.VMEM(halves + (width,), bf16),
            pltpu.VMEM(halves + (HEAD_DIM,), bf16),
            pltpu.VMEM(halves + (HEAD_DIM,), bf16),
            pltpu.VMEM((CONV, FOLLOW, width), bf16),
            pltpu.VMEM((CONV, FOLLOW, HEAD_DIM), bf16),
            pltpu.VMEM((CONV, FOLLOW, HEAD_DIM), bf16),
            pltpu.VMEM((CTX, 2, CHUNK, HEAD_DIM), bf16),
            pltpu.VMEM((CTX, 2, CHUNK, HEAD_DIM), bf16),
            pltpu.VMEM((CONV, CTX, CHUNK, HEAD_DIM), bf16),
            pltpu.VMEM((3, HALF, HEAD_DIM), bf16),
            pltpu.VMEM((PROMPT_TILE, HEAD_DIM), bf16),
            pltpu.VMEM((FOLLOW_TILE, HEAD_DIM), bf16),
            pltpu.VMEM((1 + CONV + len(REST_TILES), GROUP * HALF, HEAD_DIM), f32),
            pltpu.VMEM((1 + CONV + len(REST_TILES), GROUP * HALF, 2 * HEAD_DIM), f32),
            pltpu.VMEM((CONV, GROUP * FOLLOW, HEAD_DIM), f32),
            pltpu.VMEM((CONV, GROUP * FOLLOW, 2 * HEAD_DIM), f32),
            pltpu.SemaphoreType.DMA((11,)),
            pltpu.SemaphoreType.DMA((CONV, len(ALL_SENDS))),
            pltpu.SemaphoreType.DMA((CONV, len(ALL_SENDS))),
        ],
        compiler_params=pltpu.CompilerParams(
            collective_id=0, has_side_effects=True, vmem_limit_bytes=61 << 20
        ),
        cost_estimate=pl.CostEstimate(
            flops=7_400_000_000, bytes_accessed=8_000_000, transcendentals=15_000_000
        ),
    )(
        lengths,
        block_order,
        q_prompt.reshape(halves + (width,)),
        k_prompt.reshape(halves + (HEAD_DIM,)),
        v_prompt.reshape(halves + (HEAD_DIM,)),
        q_follow,
        k_follow,
        v_follow,
    )
    return out.reshape(q_prompt.shape), out_follow


def solution(mesh):
    return jax.shard_map(
        on_device,
        mesh=mesh,
        in_specs=(P("dp", "ctx", "tp"),) * 6 + (P("dp", None), P("dp", None)),
        out_specs=(P("dp", "ctx", "tp"), P("dp", "ctx", "tp")),
        check_vma=False,
    )
```
